32 devices in a mesh: seq: 16 (over z, y, core), dp: 2 (over x).
Axes of the slice: x: 2, y: 2, z: 4, core: 2. Of those that a mesh axis runs over, the one named last changes fastest.
Arguments:
- features: float32 [2, 4096, 512], P('dp', 'seq'), may hold values from -64 to 64
- norm_gain: float32 [2, 512], replicated, may hold values from 0.25 to 1.75
- filters: float32 [4, 512], replicated, may hold values from -1 to 1
- level_weights: float32 [13, 512], replicated, may hold values from -1.2 to 1.2
- glu_weight: float32 [512, 1024], P('dp'), may hold values from -0.25 to 0.25
- expand_weight: float32 [512, 2048], P('dp'), may hold values from -0.25 to 0.25
- reduce_weight: float32 [2048, 512], P('dp'), may hold values from -0.125 to 0.125
Outputs:
- layer_out: float32 [2, 4096, 512], P('dp', 'seq')
The draws below stay inside these ranges and needn't reach their ends.
All inputs are finite; a program needn't handle non-finite values.
Results may differ from the reference program's by a relative error of at most 0.000069.
Values sent between devices are 32-bit elements; how exact they have to be, the bound alone decides.
A program may use at most 64 MiB of HBM per device.

```python
import math
import jax
import jax.numpy as jnp
from jax import lax

D = 512
FF = 2048
LEVELS = 12
SEQ = 4096
BATCH = 2


def draw_features(key, part):
    key_base, key_rows, key_cols = jax.random.split(key, 3)
    base = jax.random.truncated_normal(key_base, -4.0, 4.0, (BATCH, SEQ, D), jnp.float32)
    row_scale = jnp.exp(jax.random.uniform(key_rows, (BATCH, SEQ, 1), jnp.float32, math.log(0.4), math.log(4.0)))
    col_scale = jnp.exp(jax.random.uniform(key_cols, (D,), jnp.float32, math.log(0.4), math.log(4.0)))
    return base * row_scale * col_scale


def draw_filters(key, part):
    angles = jax.random.uniform(key, (2, D), jnp.float32, -math.pi, math.pi)
    return jnp.stack([jnp.cos(angles[0]), jnp.sin(angles[0]), jnp.cos(angles[1]), jnp.sin(angles[1])], axis=0)


def block_levels(key, dims, cuts, least, largest):
    level, own = 1.0, jax.random.fold_in(key, 6)
    for position, parts in cuts:
        heights = jnp.exp(jax.random.uniform(jax.random.fold_in(own, position), (parts,), jnp.float32, least / len(cuts), largest / len(cuts)))
        level = level * jnp.repeat(heights, dims[position] // parts).reshape([-1 if axis == position else 1 for axis in range(len(dims))])
    return level


def scatter_about(stream_key, dims, deviation, most, shards=(), dtype=jnp.bfloat16):
    gain = block_levels(stream_key, dims, shards, -0.22, 0.18) if shards else 1.0
    result = jax.random.normal(stream_key, dims, jnp.float32) * deviation * gain
    return jnp.minimum(jnp.maximum(result, -most), most).astype(dtype)


def setup_inputs(seed: int = 0) -> dict:
    streams_of = jax.random.split(jax.random.key(seed), 8)
    features = draw_features(jax.random.fold_in(streams_of[7], 71), 0)
    norm_gain = jnp.clip(1.0 + 0.15 * jax.random.normal(streams_of[1], (2, D), jnp.float32), 0.25, 1.75)
    filters = draw_filters(jax.random.fold_in(streams_of[7], 71), 0)
    level_weights = scatter_about(streams_of[3], (LEVELS + 1, D), 0.3, 1.2, (), jnp.float32)
    glu_weight = scatter_about(streams_of[4], (D, 2 * D), D ** -0.5, 0.25, ((0, 2),), jnp.float32)
    expand_weight = scatter_about(streams_of[5], (D, FF), D ** -0.5, 0.25, ((0, 2),), jnp.float32)
    reduce_weight = scatter_about(streams_of[6], (FF, D), FF ** -0.5, 0.125, ((0, 2),), jnp.float32)
    return dict(features=features, norm_gain=norm_gain, filters=filters, level_weights=level_weights, glu_weight=glu_weight, expand_weight=expand_weight, reduce_weight=reduce_weight)


def layer_norm(values, gain_row):
    average = lax.optimization_barrier(jnp.mean(values, axis=-1, keepdims=True))
    centred = values - average
    variance = lax.optimization_barrier(jnp.mean(centred * centred, axis=-1, keepdims=True))
    return centred * lax.rsqrt(variance + 1e-05) * gain_row

def reference(features, norm_gain, filters, level_weights, glu_weight, expand_weight, reduce_weight):

    def mix_sequence(sequence):
        normed = layer_norm(sequence, norm_gain[0])
        current = normed
        detail_sum = jnp.zeros_like(normed)
        for level_step in range(LEVELS):
            spacing = 2 ** level_step
            earlier = jnp.concatenate([jnp.zeros((spacing, D), jnp.float32), current[:SEQ - spacing]], axis=0)
            detail_sum = detail_sum + level_weights[level_step] * (filters[2] * earlier + filters[3] * current)
            current = filters[0] * earlier + filters[1] * current
        detail_sum = detail_sum + level_weights[LEVELS] * current
        activated = jax.nn.gelu(detail_sum, approximate=False)
        projected = jnp.dot(activated, glu_weight, precision=lax.Precision.HIGHEST, preferred_element_type=jnp.float32)
        residual = sequence + projected[:, :D] * jax.nn.sigmoid(projected[:, D:])
        second = layer_norm(residual, norm_gain[1])
        hidden = jax.nn.relu(jnp.dot(second, expand_weight, precision=lax.Precision.HIGHEST, preferred_element_type=jnp.float32))
        return residual + jnp.dot(hidden, reduce_weight, precision=lax.Precision.HIGHEST, preferred_element_type=jnp.float32)
    return lax.map(mix_sequence, features)
```

```python
import functools

import jax
import jax.numpy as jnp
from jax import lax
from jax.experimental import pallas as pl
from jax.experimental.pallas import tpu as pltpu
from jax.sharding import PartitionSpec as P

MESH = pl.DeviceIdType.MESH
LANES = 128
CHUNKS = 2
TILE = 256


def split(v):
    hi = v.astype(jnp.bfloat16)
    return hi, (v - hi.astype(jnp.float32)).astype(jnp.bfloat16)


def dot3(a_hi, a_lo, b):
    b_hi, b_lo = split(b)
    f = functools.partial(jnp.dot, preferred_element_type=jnp.float32)
    return f(a_hi, b_hi) + (f(a_hi, b_lo) + f(a_lo, b_hi))


def norm_rows(v, gain_row):
    centred = v - jnp.mean(v, axis=-1, keepdims=True)
    variance = jnp.mean(centred * centred, axis=-1, keepdims=True)
    return centred * lax.rsqrt(variance + 1e-05) * gain_row


def kernel(
    n_seq, n_dp, rows, splits,
    x_ref, gain_ref, taps_ref, lw_ref, glu_ref, expand_ref, reduce_ref, out_ref,
    window, level, local, recv1, send2, deep, a_hi_ref, a_lo_ref,
    glu_full, expand_full, reduce_full,
    halo_s, halo_r, a1_s, a1_r, a2_s, a2_r, own_sem, w_s, w_r, w_own,
):
    extent, channels = x_ref.shape
    shallow = extent.bit_length() - 1
    deep_levels = n_seq.bit_length() - 1
    all_levels = shallow + deep_levels
    me = lax.axis_index("seq")
    my_dp = lax.axis_index("dp")
    sibling = me + 1 - 2 * lax.rem(me, 2)
    pair = me + 2 - 4 * lax.rem(me // 2, 2)
    g = lax.rem(me, 4)
    owner_width = channels // splits
    cw = owner_width // CHUNKS
    hw = channels // CHUNKS

    def seq_peer(o):
        return lax.rem(me + o, n_seq)

    def dp_peer(o):
        return lax.rem(my_dp + o, n_dp)

    barrier = pltpu.get_barrier_semaphore()

    @pl.loop(1, n_seq)
    def _(o):
        pl.semaphore_signal(barrier, inc=1, device_id={"seq": seq_peer(o)}, device_id_type=MESH)

    for o in range(1, n_dp):
        pl.semaphore_signal(barrier, inc=1, device_id={"dp": dp_peer(o)}, device_id_type=MESH)

    weights = ((glu_ref, glu_full), (expand_ref, expand_full), (reduce_ref, reduce_full))
    for w, (src, full) in enumerate(weights):
        height = src.shape[0]
        at = pl.multiple_of(my_dp * height, height)
        pltpu.make_async_copy(src, full.at[pl.ds(at, height)], w_own.at[w]).start()

    @pl.loop(0, extent // 64)
    def _(i):
        at = pl.ds(pl.multiple_of(i * 64, 64), 64)
        to = pl.ds(pl.multiple_of(extent + i * 64, 64), 64)
        window[to, :] = norm_rows(x_ref[at, :], gain_ref[0:1, :])

    @pl.when(me == 0)
    def _():
        window[0:extent, :] = jnp.zeros((extent, channels), jnp.float32)

    pl.semaphore_wait(barrier, n_seq - 1 + n_dp - 1)

    def halo(h):
        cols = slice(h * hw, (h + 1) * hw)
        return pltpu.make_async_remote_copy(
            src_ref=window.at[extent : 2 * extent, cols],
            dst_ref=window.at[0:extent, cols],
            send_sem=halo_s.at[h], recv_sem=halo_r.at[h],
            device_id={"seq": lax.rem(me + 1, n_seq)}, device_id_type=MESH,
        )

    @pl.when(me < n_seq - 1)
    def _():
        for h in range(CHUNKS):
            halo(h).start()

    def piece_rows(w, shard, k):
        height = weights[w][0].shape[0]
        part = height // 4
        return pl.ds(pl.multiple_of(shard * height + k * part, part), part)

    def over_dp(w, o):
        src, full = weights[w]
        part = src.shape[0] // 4
        return pltpu.make_async_remote_copy(
            src_ref=src.at[pl.ds(pl.multiple_of(g * part, part), part)],
            dst_ref=full.at[piece_rows(w, my_dp, g)],
            send_sem=w_s.at[w, o - 1, 0], recv_sem=w_r.at[w, o - 1, 0],
            device_id={"dp": dp_peer(o)}, device_id_type=MESH,
        )

    def forward(w, o, kind):
        full = weights[w][1]
        shard = lax.rem(my_dp + n_dp - o, n_dp)
        piece = lax.rem(g + 2, 4) if kind == 3 else g
        at = full.at[piece_rows(w, shard, piece)]
        return pltpu.make_async_remote_copy(
            src_ref=at, dst_ref=at,
            send_sem=w_s.at[w, o - 1, kind], recv_sem=w_r.at[w, o - 1, kind],
            device_id={"seq": pair if kind == 1 else sibling}, device_id_type=MESH,
        )

    offsets = range(1, n_dp)

    def stage1(w):
        for o in offsets:
            over_dp(w, o).wait_recv()
            forward(w, o, 1).start()
            forward(w, o, 2).start()

    def stage2(w):
        for o in offsets:
            forward(w, o, 1).wait_recv()
            forward(w, o, 3).start()

    def stage3(w):
        src, full = weights[w]
        for o in offsets:
            forward(w, o, 2).wait_recv()
            forward(w, o, 3).wait_recv()
        height = src.shape[0]
        at = pl.multiple_of(my_dp * height, height)
        pltpu.make_async_copy(src, full.at[pl.ds(at, height)], w_own.at[w]).wait()

    for w in range(3):
        for o in offsets:
            over_dp(w, o).start()

    def block_of(ref, owner, h):
        at = pl.multiple_of((owner // splits) * rows, rows)
        if splits == 1:
            return ref.at[pl.ds(at, rows), h * cw : (h + 1) * cw]
        lane = pl.multiple_of(lax.rem(owner, splits) * owner_width + h * cw, LANES)
        return ref.at[pl.ds(at, rows), pl.ds(lane, cw)]

    def out1(h, dest):
        return pltpu.make_async_remote_copy(
            src_ref=block_of(level, dest, h), dst_ref=recv1.at[h, me],
            send_sem=a1_s.at[h, dest], recv_sem=a1_r.at[h, me],
            device_id={"seq": dest}, device_id_type=MESH,
        )

    def in1(h, source):
        return pltpu.make_async_remote_copy(
            src_ref=block_of(level, source, h), dst_ref=recv1.at[h, source],
            send_sem=a1_s.at[h, source], recv_sem=a1_r.at[h, source],
            device_id={"seq": source}, device_id_type=MESH,
        )

    def out2(h, dest):
        return pltpu.make_async_remote_copy(
            src_ref=send2.at[h, dest], dst_ref=block_of(deep, me, h),
            send_sem=a2_s.at[h, dest], recv_sem=a2_r.at[h, me],
            device_id={"seq": dest}, device_id_type=MESH,
        )

    def in2(h, source):
        return pltpu.make_async_remote_copy(
            src_ref=send2.at[h, source], dst_ref=block_of(deep, source, h),
            send_sem=a2_s.at[h, source], recv_sem=a2_r.at[h, source],
            device_id={"seq": source}, device_id_type=MESH,
        )

    for h in range(CHUNKS):

        @pl.when(me > 0)
        def _():
            halo(h).wait_recv()

        @pl.loop(0, hw // LANES)
        def _(c):
            lanes = pl.ds(pl.multiple_of(h * hw + c * LANES, LANES), LANES)
            tap = [taps_ref[i : i + 1, lanes] for i in range(4)]
            current = window[:, lanes]
            total = jnp.zeros((extent, LANES), jnp.float32)
            for step in range(shallow):
                earlier = pltpu.roll(current, 2**step, 0)
                weight = lw_ref[step : step + 1, lanes]
                total = total + (
                    (weight * tap[2]) * earlier[extent:] + (weight * tap[3]) * current[extent:]
                )
                current = tap[0] * earlier + tap[1] * current
            level[:, lanes] = current[extent:]
            local[:, lanes] = total

        own = pltpu.make_async_copy(block_of(level, me, h), recv1.at[h, me], own_sem.at[h])
        own.start()

        @pl.loop(1, n_seq)
        def _(o):
            out1(h, seq_peer(o)).start()

        own.wait()

    stage1(0)

    for h in range(CHUNKS):

        @pl.loop(1, n_seq)
        def _(o):
            in1(h, seq_peer(o)).wait_recv()

        @pl.loop(0, cw // LANES)
        def _(c):
            lanes = pl.ds(pl.multiple_of(c * LANES, LANES), LANES)
            first = h * cw + c * LANES
            if splits > 1:
                first = lax.rem(me, splits) * owner_width + first
            at = pl.ds(pl.multiple_of(first, LANES), LANES)
            tap = [taps_ref[i : i + 1, at][None] for i in range(4)]
            current = recv1[h, :, :, lanes]
            total = jnp.zeros_like(current)
            for step in range(deep_levels):
                shift = 2**step
                earlier = jnp.concatenate(
                    [jnp.zeros((shift, rows, LANES), jnp.float32), current[: n_seq - shift]], axis=0
                )
                weight = lw_ref[shallow + step : shallow + step + 1, at][None]
                total = total + (weight * tap[2]) * earlier + (weight * tap[3]) * current
                current = tap[0] * earlier + tap[1] * current
            total = total + lw_ref[all_levels : all_levels + 1, at][None] * current
            send2[h, :, :, lanes] = total

        own = pltpu.make_async_copy(send2.at[h, me], block_of(deep, me, h), own_sem.at[h])
        own.start()

        @pl.loop(1, n_seq)
        def _(o):
            out2(h, seq_peer(o)).start()

        own.wait()

    stage2(0)
    stage1(1)
    stage2(1)
    stage1(2)

    for h in range(CHUNKS):

        @pl.loop(1, n_seq)
        def _(o):
            in2(h, seq_peer(o)).wait_recv()

    @pl.loop(0, extent // 64)
    def _(i):
        at = pl.ds(pl.multiple_of(i * 64, 64), 64)
        v = local[at, :] + deep[at, :]
        hi, lo = split(0.5 * v * (1.0 + lax.erf(v * 0.7071067811865476)))
        a_hi_ref[at, :] = hi
        a_lo_ref[at, :] = lo

    stage3(0)

    @pl.loop(0, channels // TILE)
    def _(t):
        at = pl.ds(pl.multiple_of(t * TILE, TILE), TILE)
        gate_at = pl.ds(pl.multiple_of(channels + t * TILE, TILE), TILE)
        value = dot3(a_hi_ref[...], a_lo_ref[...], glu_full[:, at])
        gate = dot3(a_hi_ref[...], a_lo_ref[...], glu_full[:, gate_at])
        out_ref[:, at] = x_ref[:, at] + value * jax.nn.sigmoid(gate)

    stage2(2)

    @pl.loop(0, extent // 64)
    def _(i):
        at = pl.ds(pl.multiple_of(i * 64, 64), 64)
        hi, lo = split(norm_rows(out_ref[at, :], gain_ref[1:2, :]))
        a_hi_ref[at, :] = hi
        a_lo_ref[at, :] = lo

    stage3(1)
    stage3(2)

    @pl.loop(0, expand_full.shape[1] // TILE)
    def _(t):
        at = pl.ds(pl.multiple_of(t * TILE, TILE), TILE)
        hidden = jnp.maximum(dot3(a_hi_ref[...], a_lo_ref[...], expand_full[:, at]), 0.0)
        hi, lo = split(hidden)
        out_ref[...] += dot3(hi, lo, reduce_full[at, :])

    @pl.when(me < n_seq - 1)
    def _():
        for h in range(CHUNKS):
            halo(h).wait_send()

    for h in range(CHUNKS):

        @pl.loop(1, n_seq)
        def _(o):
            out1(h, seq_peer(o)).wait_send()
            out2(h, seq_peer(o)).wait_send()

    for w in range(3):
        for o in offsets:
            over_dp(w, o).wait_send()
            for kind in (1, 2, 3):
                forward(w, o, kind).wait_send()


def body(n_seq, n_dp, features, norm_gain, filters, level_weights, glu, expand, reduce):
    batches, extent, channels = features.shape
    rows = max(8, extent // n_seq)
    splits = n_seq * rows // extent
    cw = channels // splits // CHUNKS
    f32 = jnp.float32
    vmem = pl.BlockSpec(memory_space=pltpu.VMEM)
    hbm = pl.BlockSpec(memory_space=pl.ANY)
    dma = pltpu.SemaphoreType.DMA
    ff = expand.shape[1]
    out = pl.pallas_call(
        functools.partial(kernel, n_seq, n_dp, rows, splits),
        out_shape=jax.ShapeDtypeStruct((extent, channels), f32),
        in_specs=[vmem] * 4 + [hbm] * 3,
        out_specs=vmem,
        scratch_shapes=[
            pltpu.VMEM((2 * extent, channels), f32),
            pltpu.VMEM((extent, channels), f32),
            pltpu.VMEM((extent, channels), f32),
            pltpu.VMEM((CHUNKS, n_seq, rows, cw), f32),
            pltpu.VMEM((CHUNKS, n_seq, rows, cw), f32),
            pltpu.VMEM((extent, channels), f32),
            pltpu.VMEM((extent, channels), jnp.bfloat16),
            pltpu.VMEM((extent, channels), jnp.bfloat16),
            pltpu.VMEM((glu.shape[0] * n_dp, glu.shape[1]), f32),
            pltpu.VMEM((expand.shape[0] * n_dp, ff), f32),
            pltpu.VMEM((reduce.shape[0] * n_dp, channels), f32),
            dma((CHUNKS,)), dma((CHUNKS,)),
            dma((CHUNKS, n_seq)), dma((CHUNKS, n_seq)),
            dma((CHUNKS, n_seq)), dma((CHUNKS, n_seq)),
            dma((CHUNKS,)),
            dma((3, n_dp - 1, 4)), dma((3, n_dp - 1, 4)),
            dma((3,)),
        ],
        compiler_params=pltpu.CompilerParams(
            collective_id=0, has_side_effects=True, vmem_limit_bytes=44 * 1024 * 1024
        ),
        cost_estimate=pl.CostEstimate(
            flops=6 * extent * channels * (2 * channels + 2 * ff),
            bytes_accessed=4 * (3 * extent * channels), transcendentals=extent * channels * 2,
        ),
    )(features.reshape(extent, channels), norm_gain, filters, level_weights, glu, expand, reduce)
    return out.reshape(batches, extent, channels)


def solution(mesh):
    return jax.shard_map(
        functools.partial(body, mesh.shape["seq"], mesh.shape["dp"]),
        mesh=mesh,
        in_specs=(P("dp", "seq", None), P(), P(), P(), P("dp", None), P("dp", None), P("dp", None)),
        out_specs=P("dp", "seq", None),
        check_vma=False,
    )
```

```python
import functools

import jax
import jax.numpy as jnp
from jax import lax
from jax.experimental import pallas as pl
from jax.experimental.pallas import tpu as pltpu
from jax.sharding import PartitionSpec as P

MESH = pl.DeviceIdType.MESH
LANES = 128
CHUNKS = 2
TILE = 256


def split(v):
    hi = v.astype(jnp.bfloat16)
    return hi, (v - hi.astype(jnp.float32)).astype(jnp.bfloat16)


def dot3(a_hi, a_lo, b):
    b_hi, b_lo = split(b)
    f = functools.partial(jnp.dot, preferred_element_type=jnp.float32)
    return f(a_hi, b_hi) + (f(a_hi, b_lo) + f(a_lo, b_hi))


def norm_rows(v, gain_row):
    centred = v - jnp.mean(v, axis=-1, keepdims=True)
    variance = jnp.mean(centred * centred, axis=-1, keepdims=True)
    return centred * lax.rsqrt(variance + 1e-05) * gain_row


def kernel(
    n_seq, n_dp, rows, splits,
    x_in, gain_in, taps_in, lw_in, glu_ref, expand_ref, reduce_ref, out_ref,
    x_ref, gain_ref, taps_ref, lw_ref, window, level, local, recv1, send2, deep, a_hi_ref, a_lo_ref,
    glu_full, expand_full, reduce_full,
    halo_s, halo_r, a1_s, a1_r, a2_s, a2_r, own_sem, w_s, w_r, w_own, in_sem,
):
    extent, channels = x_ref.shape
    shallow = extent.bit_length() - 1
    deep_levels = n_seq.bit_length() - 1
    all_levels = shallow + deep_levels
    me = lax.axis_index("seq")
    my_dp = lax.axis_index("dp")
    sibling = me + 1 - 2 * lax.rem(me, 2)
    pair = me + 2 - 4 * lax.rem(me // 2, 2)
    g = lax.rem(me, 4)
    hw = channels // CHUNKS
    cw = hw // splits

    def seq_peer(o):
        return lax.rem(me + o, n_seq)

    def dp_peer(o):
        return lax.rem(my_dp + o, n_dp)

    inputs = ((x_in, x_ref), (gain_in, gain_ref), (taps_in, taps_ref), (lw_in, lw_ref))
    copies = [pltpu.make_async_copy(a, b, in_sem.at[i]) for i, (a, b) in enumerate(inputs)]
    for copy in copies:
        copy.start()

    barrier = pltpu.get_barrier_semaphore()

    @pl.loop(1, n_seq)
    def _(o):
        pl.semaphore_signal(barrier, inc=1, device_id={"seq": seq_peer(o)}, device_id_type=MESH)

    for o in range(1, n_dp):
        pl.semaphore_signal(barrier, inc=1, device_id={"dp": dp_peer(o)}, device_id_type=MESH)

    weights = ((glu_ref, glu_full, 4), (expand_ref, expand_full, 4), (reduce_ref, reduce_full, 2))

    def own_shard(w):
        src, full, _ = weights[w]
        height = src.shape[0]
        at = pl.multiple_of(my_dp * height, height)
        return pltpu.make_async_copy(src, full.at[pl.ds(at, height)], w_own.at[w])

    for copy in copies:
        copy.wait()

    @pl.loop(0, extent // 64)
    def _(i):
        at = pl.ds(pl.multiple_of(i * 64, 64), 64)
        to = pl.ds(pl.multiple_of(extent + i * 64, 64), 64)
        window[to, :] = norm_rows(x_ref[at, :], gain_ref[0:1, :])

    @pl.when(me == 0)
    def _():
        window[0:extent, :] = jnp.zeros((extent, channels), jnp.float32)

    pl.semaphore_wait(barrier, n_seq - 1 + n_dp - 1)

    def halo(h):
        cols = slice(h * hw, (h + 1) * hw)
        return pltpu.make_async_remote_copy(
            src_ref=window.at[extent : 2 * extent, cols],
            dst_ref=window.at[0:extent, cols],
            send_sem=halo_s.at[h], recv_sem=halo_r.at[h],
            device_id={"seq": lax.rem(me + 1, n_seq)}, device_id_type=MESH,
        )

    @pl.when(me < n_seq - 1)
    def _():
        for h in range(CHUNKS):
            halo(h).start()

    def piece_rows(w, shard, k):
        height = weights[w][0].shape[0]
        part = height // weights[w][2]
        return pl.ds(pl.multiple_of(shard * height + k * part, part), part)

    def over_dp(w, o):
        src, full, pieces = weights[w]
        part = src.shape[0] // pieces
        mine = lax.rem(g, pieces)
        return pltpu.make_async_remote_copy(
            src_ref=src.at[pl.ds(pl.multiple_of(mine * part, part), part)],
            dst_ref=full.at[piece_rows(w, my_dp, mine)],
            send_sem=w_s.at[w, o - 1, 0], recv_sem=w_r.at[w, o - 1, 0],
            device_id={"dp": dp_peer(o)}, device_id_type=MESH,
        )

    def forward(w, o, kind):
        full = weights[w][1]
        shard = lax.rem(my_dp + n_dp - o, n_dp)
        piece = lax.rem(g + 2, 4) if kind == 3 else lax.rem(g, weights[w][2])
        at = full.at[piece_rows(w, shard, piece)]
        return pltpu.make_async_remote_copy(
            src_ref=at, dst_ref=at,
            send_sem=w_s.at[w, o - 1, kind], recv_sem=w_r.at[w, o - 1, kind],
            device_id={"seq": pair if kind == 1 else sibling}, device_id_type=MESH,
        )

    offsets = range(1, n_dp)

    def stage1(w):
        for o in offsets:
            over_dp(w, o).wait_recv()
            if weights[w][2] == 4:
                forward(w, o, 1).start()
            forward(w, o, 2).start()

    def stage2(w):
        for o in offsets:
            forward(w, o, 1).wait_recv()
            forward(w, o, 3).start()

    def stage3(w):
        for o in offsets:
            forward(w, o, 2).wait_recv()
            if weights[w][2] == 4:
                forward(w, o, 3).wait_recv()

    def send_over_dp(w):
        for o in offsets:
            over_dp(w, o).start()

    send_over_dp(0)
    send_over_dp(1)
    for w in range(3):
        own_shard(w).start()

    def block_of(ref, owner, h):
        at = pl.multiple_of((owner // splits) * rows, rows)
        if splits == 1:
            return ref.at[pl.ds(at, rows), h * cw : (h + 1) * cw]
        lane = pl.multiple_of(h * hw + lax.rem(owner, splits) * cw, LANES)
        return ref.at[pl.ds(at, rows), pl.ds(lane, cw)]

    def out1(h, dest):
        return pltpu.make_async_remote_copy(
            src_ref=block_of(level, dest, h), dst_ref=recv1.at[h, me],
            send_sem=a1_s.at[h, dest], recv_sem=a1_r.at[h, me],
            device_id={"seq": dest}, device_id_type=MESH,
        )

    def in1(h, source):
        return pltpu.make_async_remote_copy(
            src_ref=block_of(level, source, h), dst_ref=recv1.at[h, source],
            send_sem=a1_s.at[h, source], recv_sem=a1_r.at[h, source],
            device_id={"seq": source}, device_id_type=MESH,
        )

    def out2(h, dest):
        return pltpu.make_async_remote_copy(
            src_ref=send2.at[h, dest], dst_ref=block_of(deep, me, h),
            send_sem=a2_s.at[h, dest], recv_sem=a2_r.at[h, me],
            device_id={"seq": dest}, device_id_type=MESH,
        )

    def in2(h, source):
        return pltpu.make_async_remote_copy(
            src_ref=send2.at[h, source], dst_ref=block_of(deep, source, h),
            send_sem=a2_s.at[h, source], recv_sem=a2_r.at[h, source],
            device_id={"seq": source}, device_id_type=MESH,
        )

    for h in range(CHUNKS):

        @pl.when(me > 0)
        def _():
            halo(h).wait_recv()

        @pl.loop(0, hw // LANES)
        def _(c):
            lanes = pl.ds(pl.multiple_of(h * hw + c * LANES, LANES), LANES)
            tap = [taps_ref[i : i + 1, lanes] for i in range(4)]
            current = window[:, lanes]
            total = jnp.zeros((extent, LANES), jnp.float32)
            for step in range(shallow):
                earlier = pltpu.roll(current, 2**step, 0)
                weight = lw_ref[step : step + 1, lanes]
                total = total + (
                    (weight * tap[2]) * earlier[extent:] + (weight * tap[3]) * current[extent:]
                )
                current = tap[0] * earlier + tap[1] * current
            level[:, lanes] = current[extent:]
            local[:, lanes] = total

        own = pltpu.make_async_copy(block_of(level, me, h), recv1.at[h, me], own_sem.at[h])
        own.start()

        @pl.loop(1, n_seq)
        def _(o):
            out1(h, seq_peer(o)).start()

        own.wait()

    stage1(0)
    send_over_dp(2)

    for h in range(CHUNKS):

        @pl.loop(1, n_seq)
        def _(o):
            in1(h, seq_peer(o)).wait_recv()

        @pl.loop(0, cw // LANES)
        def _(c):
            lanes = pl.ds(pl.multiple_of(c * LANES, LANES), LANES)
            first = h * hw + c * LANES
            if splits > 1:
                first = first + lax.rem(me, splits) * cw
            at = pl.ds(pl.multiple_of(first, LANES), LANES)
            tap = [taps_ref[i : i + 1, at][None] for i in range(4)]
            current = recv1[h, :, :, lanes]
            total = jnp.zeros_like(current)
            for step in range(deep_levels):
                shift = 2**step
                earlier = jnp.concatenate(
                    [jnp.zeros((shift, rows, LANES), jnp.float32), current[: n_seq - shift]], axis=0
                )
                weight = lw_ref[shallow + step : shallow + step + 1, at][None]
                total = total + (weight * tap[2]) * earlier + (weight * tap[3]) * current
                current = tap[0] * earlier + tap[1] * current
            total = total + lw_ref[all_levels : all_levels + 1, at][None] * current
            send2[h, :, :, lanes] = total

        own = pltpu.make_async_copy(send2.at[h, me], block_of(deep, me, h), own_sem.at[h])
        own.start()

        @pl.loop(1, n_seq)
        def _(o):
            out2(h, seq_peer(o)).start()

        own.wait()
        if h == 0:
            stage2(0)
            stage1(1)

    stage2(1)

    for h in range(CHUNKS):

        @pl.loop(1, n_seq)
        def _(o):
            in2(h, seq_peer(o)).wait_recv()

    @pl.loop(0, extent // 64)
    def _(i):
        at = pl.ds(pl.multiple_of(i * 64, 64), 64)
        v = local[at, :] + deep[at, :]
        hi, lo = split(0.5 * v * (1.0 + lax.erf(v * 0.7071067811865476)))
        a_hi_ref[at, :] = hi
        a_lo_ref[at, :] = lo

    own_shard(0).wait()
    stage3(0)

    @pl.loop(0, channels // TILE)
    def _(t):
        at = pl.ds(pl.multiple_of(t * TILE, TILE), TILE)
        gate_at = pl.ds(pl.multiple_of(channels + t * TILE, TILE), TILE)
        value = dot3(a_hi_ref[...], a_lo_ref[...], glu_full[:, at])
        gate = dot3(a_hi_ref[...], a_lo_ref[...], glu_full[:, gate_at])
        out_ref[:, at] = x_ref[:, at] + value * jax.nn.sigmoid(gate)

    stage1(2)

    @pl.loop(0, extent // 64)
    def _(i):
        at = pl.ds(pl.multiple_of(i * 64, 64), 64)
        hi, lo = split(norm_rows(out_ref[at, :], gain_ref[1:2, :]))
        a_hi_ref[at, :] = hi
        a_lo_ref[at, :] = lo

    own_shard(1).wait()
    own_shard(2).wait()
    stage3(1)

    def feed_forward(shard):
        height = reduce_ref.shape[0]

        @pl.loop(0, height // TILE)
        def _(t):
            at = pl.ds(pl.multiple_of(shard * height + t * TILE, TILE), TILE)
            hidden = jnp.maximum(dot3(a_hi_ref[...], a_lo_ref[...], expand_full[:, at]), 0.0)
            hi, lo = split(hidden)
            out_ref[...] += dot3(hi, lo, reduce_full[at, :])

    feed_forward(my_dp)
    stage3(2)
    for o in offsets:
        feed_forward(dp_peer(o))

    @pl.when(me < n_seq - 1)
    def _():
        for h in range(CHUNKS):
            halo(h).wait_send()

    for h in range(CHUNKS):

        @pl.loop(1, n_seq)
        def _(o):
            out1(h, seq_peer(o)).wait_send()
            out2(h, seq_peer(o)).wait_send()

    for w in range(3):
        for o in offsets:
            over_dp(w, o).wait_send()
            for kind in (1, 2, 3) if weights[w][2] == 4 else (2,):
                forward(w, o, kind).wait_send()


def body(n_seq, n_dp, features, norm_gain, filters, level_weights, glu, expand, reduce):
    batches, extent, channels = features.shape
    rows = max(8, extent // n_seq)
    splits = n_seq * rows // extent
    cw = channels // splits // CHUNKS
    f32 = jnp.float32
    vmem = pl.BlockSpec(memory_space=pltpu.VMEM)
    hbm = pl.BlockSpec(memory_space=pl.ANY)
    dma = pltpu.SemaphoreType.DMA
    ff = expand.shape[1]
    out = pl.pallas_call(
        functools.partial(kernel, n_seq, n_dp, rows, splits),
        out_shape=jax.ShapeDtypeStruct((extent, channels), f32),
        in_specs=[hbm] * 7,
        out_specs=vmem,
        scratch_shapes=[
            pltpu.VMEM((extent, channels), f32),
            pltpu.VMEM(norm_gain.shape, f32),
            pltpu.VMEM(filters.shape, f32),
            pltpu.VMEM(level_weights.shape, f32),
            pltpu.VMEM((2 * extent, channels), f32),
            pltpu.VMEM((extent, channels), f32),
            pltpu.VMEM((extent, channels), f32),
            pltpu.VMEM((CHUNKS, n_seq, rows, cw), f32),
            pltpu.VMEM((CHUNKS, n_seq, rows, cw), f32),
            pltpu.VMEM((extent, channels), f32),
            pltpu.VMEM((extent, channels), jnp.bfloat16),
            pltpu.VMEM((extent, channels), jnp.bfloat16),
            pltpu.VMEM((glu.shape[0] * n_dp, glu.shape[1]), f32),
            pltpu.VMEM((expand.shape[0] * n_dp, ff), f32),
            pltpu.VMEM((reduce.shape[0] * n_dp, channels), f32),
            dma((CHUNKS,)), dma((CHUNKS,)),
            dma((CHUNKS, n_seq)), dma((CHUNKS, n_seq)),
            dma((CHUNKS, n_seq)), dma((CHUNKS, n_seq)),
            dma((CHUNKS,)),
            dma((3, n_dp - 1, 4)), dma((3, n_dp - 1, 4)),
            dma((3,)), dma((4,)),
        ],
        compiler_params=pltpu.CompilerParams(
            collective_id=0, has_side_effects=True, vmem_limit_bytes=60 * 1024 * 1024
        ),
        cost_estimate=pl.CostEstimate(
            flops=6 * extent * channels * (2 * channels + 2 * ff),
            bytes_accessed=4 * (3 * extent * channels), transcendentals=extent * channels * 2,
        ),
    )(features.reshape(extent, channels), norm_gain, filters, level_weights, glu, expand, reduce)
    return out.reshape(batches, extent, channels)


def solution(mesh):
    return jax.shard_map(
        functools.partial(body, mesh.shape["seq"], mesh.shape["dp"]),
        mesh=mesh,
        in_specs=(P("dp", "seq", None), P(), P(), P(), P("dp", None), P("dp", None), P("dp", None)),
        out_specs=P("dp", "seq", None),
        check_vma=False,
    )
```

```python
import functools

import jax
import jax.numpy as jnp
from jax import lax
from jax.experimental import pallas as pl
from jax.experimental.pallas import tpu as pltpu
from jax.sharding import PartitionSpec as P

MESH = pl.DeviceIdType.MESH
LANES = 128
CHUNKS = 2
TILE = 256


def split(v):
    hi = v.astype(jnp.bfloat16)
    return hi, (v - hi.astype(jnp.float32)).astype(jnp.bfloat16)


def dot3(a_hi, a_lo, b):
    b_hi, b_lo = split(b)
    f = functools.partial(jnp.dot, preferred_element_type=jnp.float32)
    return f(a_hi, b_hi) + (f(a_hi, b_lo) + f(a_lo, b_hi))


def norm_rows(v, gain_row):
    centred = v - jnp.mean(v, axis=-1, keepdims=True)
    variance = jnp.mean(centred * centred, axis=-1, keepdims=True)
    return centred * lax.rsqrt(variance + 1e-05) * gain_row


def kernel(
    n_seq, n_dp, rows, splits,
    x_in, gain_in, taps_in, lw_in, glu_ref, expand_ref, reduce_ref, out_ref,
    x_ref, gain_ref, taps_ref, lw_ref, window, level, local, recv1, send2, deep, a_hi_ref, a_lo_ref,
    glu_full, expand_full, reduce_full, proj,
    halo_s, halo_r, a1_s, a1_r, a2_s, a2_r, own_sem, w_s, w_r, w_own, in_sem,
):
    extent, channels = x_ref.shape
    shallow = extent.bit_length() - 1
    deep_levels = n_seq.bit_length() - 1
    all_levels = shallow + deep_levels
    me = lax.axis_index("seq")
    my_dp = lax.axis_index("dp")
    sibling = me + 1 - 2 * lax.rem(me, 2)
    pair = me + 2 - 4 * lax.rem(me // 2, 2)
    g = lax.rem(me, 4)
    hw = channels // CHUNKS
    cw = hw // splits

    def seq_peer(o):
        return lax.rem(me + o, n_seq)

    def dp_peer(o):
        return lax.rem(my_dp + o, n_dp)

    inputs = ((x_in, x_ref), (gain_in, gain_ref), (taps_in, taps_ref), (lw_in, lw_ref))
    copies = [pltpu.make_async_copy(a, b, in_sem.at[i]) for i, (a, b) in enumerate(inputs)]
    for copy in copies:
        copy.start()

    barrier = pltpu.get_barrier_semaphore()

    @pl.loop(1, n_seq)
    def _(o):
        pl.semaphore_signal(barrier, inc=1, device_id={"seq": seq_peer(o)}, device_id_type=MESH)

    for o in range(1, n_dp):
        pl.semaphore_signal(barrier, inc=1, device_id={"dp": dp_peer(o)}, device_id_type=MESH)

    weights = ((glu_ref, glu_full, 4), (expand_ref, expand_full, 4), (reduce_ref, reduce_full, 2))

    def own_shard(w):
        src, full, _ = weights[w]
        height = src.shape[0]
        at = pl.multiple_of(my_dp * height, height)
        return pltpu.make_async_copy(src, full.at[pl.ds(at, height)], w_own.at[w])

    for copy in copies:
        copy.wait()

    @pl.loop(0, extent // 64)
    def _(i):
        at = pl.ds(pl.multiple_of(i * 64, 64), 64)
        to = pl.ds(pl.multiple_of(extent + i * 64, 64), 64)
        window[to, :] = norm_rows(x_ref[at, :], gain_ref[0:1, :])

    @pl.when(me == 0)
    def _():
        window[0:extent, :] = jnp.zeros((extent, channels), jnp.float32)

    pl.semaphore_wait(barrier, n_seq - 1 + n_dp - 1)

    def halo(h):
        cols = slice(h * hw, (h + 1) * hw)
        return pltpu.make_async_remote_copy(
            src_ref=window.at[extent : 2 * extent, cols],
            dst_ref=window.at[0:extent, cols],
            send_sem=halo_s.at[h], recv_sem=halo_r.at[h],
            device_id={"seq": lax.rem(me + 1, n_seq)}, device_id_type=MESH,
        )

    @pl.when(me < n_seq - 1)
    def _():
        for h in range(CHUNKS):
            halo(h).start()

    def piece_rows(w, shard, k):
        height = weights[w][0].shape[0]
        part = height // weights[w][2]
        return pl.ds(pl.multiple_of(shard * height + k * part, part), part)

    def over_dp(w, o):
        src, full, pieces = weights[w]
        part = src.shape[0] // pieces
        mine = lax.rem(g, pieces)
        return pltpu.make_async_remote_copy(
            src_ref=src.at[pl.ds(pl.multiple_of(mine * part, part), part)],
            dst_ref=full.at[piece_rows(w, my_dp, mine)],
            send_sem=w_s.at[w, o - 1, 0], recv_sem=w_r.at[w, o - 1, 0],
            device_id={"dp": dp_peer(o)}, device_id_type=MESH,
        )

    def forward(w, o, kind):
        full = weights[w][1]
        shard = lax.rem(my_dp + n_dp - o, n_dp)
        piece = lax.rem(g + 2, 4) if kind == 3 else lax.rem(g, weights[w][2])
        at = full.at[piece_rows(w, shard, piece)]
        return pltpu.make_async_remote_copy(
            src_ref=at, dst_ref=at,
            send_sem=w_s.at[w, o - 1, kind], recv_sem=w_r.at[w, o - 1, kind],
            device_id={"seq": pair if kind == 1 else sibling}, device_id_type=MESH,
        )

    offsets = range(1, n_dp)

    def stage1(w):
        for o in offsets:
            over_dp(w, o).wait_recv()
            if weights[w][2] == 4:
                forward(w, o, 1).start()
            forward(w, o, 2).start()

    def stage2(w):
        for o in offsets:
            forward(w, o, 1).wait_recv()
            forward(w, o, 3).start()

    def stage3(w):
        for o in offsets:
            forward(w, o, 2).wait_recv()
            if weights[w][2] == 4:
                forward(w, o, 3).wait_recv()

    def send_over_dp(w):
        for o in offsets:
            over_dp(w, o).start()

    send_over_dp(0)
    send_over_dp(1)
    for w in range(3):
        own_shard(w).start()

    def block_of(ref, owner, h):
        at = pl.multiple_of((owner // splits) * rows, rows)
        if splits == 1:
            return ref.at[pl.ds(at, rows), h * cw : (h + 1) * cw]
        lane = pl.multiple_of(h * hw + lax.rem(owner, splits) * cw, LANES)
        return ref.at[pl.ds(at, rows), pl.ds(lane, cw)]

    def out1(h, dest):
        return pltpu.make_async_remote_copy(
            src_ref=block_of(level, dest, h), dst_ref=recv1.at[h, me],
            send_sem=a1_s.at[h, dest], recv_sem=a1_r.at[h, me],
            device_id={"seq": dest}, device_id_type=MESH,
        )

    def in1(h, source):
        return pltpu.make_async_remote_copy(
            src_ref=block_of(level, source, h), dst_ref=recv1.at[h, source],
            send_sem=a1_s.at[h, source], recv_sem=a1_r.at[h, source],
            device_id={"seq": source}, device_id_type=MESH,
        )

    def out2(h, dest):
        return pltpu.make_async_remote_copy(
            src_ref=send2.at[h, dest], dst_ref=block_of(deep, me, h),
            send_sem=a2_s.at[h, dest], recv_sem=a2_r.at[h, me],
            device_id={"seq": dest}, device_id_type=MESH,
        )

    def in2(h, source):
        return pltpu.make_async_remote_copy(
            src_ref=send2.at[h, source], dst_ref=block_of(deep, source, h),
            send_sem=a2_s.at[h, source], recv_sem=a2_r.at[h, source],
            device_id={"seq": source}, device_id_type=MESH,
        )

    for h in range(CHUNKS):

        @pl.when(me > 0)
        def _():
            halo(h).wait_recv()

        @pl.loop(0, hw // LANES)
        def _(c):
            lanes = pl.ds(pl.multiple_of(h * hw + c * LANES, LANES), LANES)
            tap = [taps_ref[i : i + 1, lanes] for i in range(4)]
            current = window[:, lanes]
            total = jnp.zeros((extent, LANES), jnp.float32)
            for step in range(shallow):
                earlier = pltpu.roll(current, 2**step, 0)
                weight = lw_ref[step : step + 1, lanes]
                total = total + (
                    (weight * tap[2]) * earlier[extent:] + (weight * tap[3]) * current[extent:]
                )
                current = tap[0] * earlier + tap[1] * current
            level[:, lanes] = current[extent:]
            local[:, lanes] = total

        own = pltpu.make_async_copy(block_of(level, me, h), recv1.at[h, me], own_sem.at[h])
        own.start()

        @pl.loop(1, n_seq)
        def _(o):
            out1(h, seq_peer(o)).start()

        own.wait()

    stage1(0)
    send_over_dp(2)

    for h in range(CHUNKS):

        @pl.loop(1, n_seq)
        def _(o):
            in1(h, seq_peer(o)).wait_recv()

        @pl.loop(0, cw // LANES)
        def _(c):
            lanes = pl.ds(pl.multiple_of(c * LANES, LANES), LANES)
            first = h * hw + c * LANES
            if splits > 1:
                first = first + lax.rem(me, splits) * cw
            at = pl.ds(pl.multiple_of(first, LANES), LANES)
            tap = [taps_ref[i : i + 1, at][None] for i in range(4)]
            current = recv1[h, :, :, lanes]
            total = jnp.zeros_like(current)
            for step in range(deep_levels):
                shift = 2**step
                earlier = jnp.concatenate(
                    [jnp.zeros((shift, rows, LANES), jnp.float32), current[: n_seq - shift]], axis=0
                )
                weight = lw_ref[shallow + step : shallow + step + 1, at][None]
                total = total + (weight * tap[2]) * earlier + (weight * tap[3]) * current
                current = tap[0] * earlier + tap[1] * current
            total = total + lw_ref[all_levels : all_levels + 1, at][None] * current
            send2[h, :, :, lanes] = total

        own = pltpu.make_async_copy(send2.at[h, me], block_of(deep, me, h), own_sem.at[h])
        own.start()

        @pl.loop(1, n_seq)
        def _(o):
            out2(h, seq_peer(o)).start()

        own.wait()
        if h == 0:
            stage2(0)
            stage1(1)

    own_shard(0).wait()
    for h in range(CHUNKS):
        cols = slice(h * hw, (h + 1) * hw)

        @pl.loop(1, n_seq)
        def _(o):
            in2(h, seq_peer(o)).wait_recv()

        @pl.loop(0, extent // 64)
        def _(i):
            at = pl.ds(pl.multiple_of(i * 64, 64), 64)
            v = local[at, cols] + deep[at, cols]
            hi, lo = split(0.5 * v * (1.0 + lax.erf(v * 0.7071067811865476)))
            a_hi_ref[at, cols] = hi
            a_lo_ref[at, cols] = lo

        if h == 0:
            stage3(0)
        if h == CHUNKS - 1:
            stage2(1)

        @pl.loop(0, channels // TILE)
        def _(t):
            at = pl.ds(pl.multiple_of(t * TILE, TILE), TILE)
            gate_at = pl.ds(pl.multiple_of(channels + t * TILE, TILE), TILE)
            value = dot3(a_hi_ref[:, cols], a_lo_ref[:, cols], glu_full[cols, at])
            gate = dot3(a_hi_ref[:, cols], a_lo_ref[:, cols], glu_full[cols, gate_at])
            if h > 0:
                value = value + proj[:, at]
                gate = gate + proj[:, gate_at]
            if h < CHUNKS - 1:
                proj[:, at] = value
                proj[:, gate_at] = gate
            else:
                out_ref[:, at] = x_ref[:, at] + value * jax.nn.sigmoid(gate)

    stage1(2)

    @pl.loop(0, extent // 64)
    def _(i):
        at = pl.ds(pl.multiple_of(i * 64, 64), 64)
        hi, lo = split(norm_rows(out_ref[at, :], gain_ref[1:2, :]))
        a_hi_ref[at, :] = hi
        a_lo_ref[at, :] = lo

    own_shard(1).wait()
    own_shard(2).wait()
    stage3(1)

    def feed_forward(shard):
        height = reduce_ref.shape[0]

        @pl.loop(0, height // TILE, unroll=min(2, height // TILE))
        def _(t):
            at = pl.ds(pl.multiple_of(shard * height + t * TILE, TILE), TILE)
            hidden = jnp.maximum(dot3(a_hi_ref[...], a_lo_ref[...], expand_full[:, at]), 0.0)
            hi, lo = split(hidden)
            out_ref[...] += dot3(hi, lo, reduce_full[at, :])

    feed_forward(my_dp)
    stage3(2)
    for o in offsets:
        feed_forward(dp_peer(o))

    @pl.when(me < n_seq - 1)
    def _():
        for h in range(CHUNKS):
            halo(h).wait_send()

    for h in range(CHUNKS):

        @pl.loop(1, n_seq)
        def _(o):
            out1(h, seq_peer(o)).wait_send()
            out2(h, seq_peer(o)).wait_send()

    for w in range(3):
        for o in offsets:
            over_dp(w, o).wait_send()
            for kind in (1, 2, 3) if weights[w][2] == 4 else (2,):
                forward(w, o, kind).wait_send()


def body(n_seq, n_dp, features, norm_gain, filters, level_weights, glu, expand, reduce):
    batches, extent, channels = features.shape
    rows = max(8, extent // n_seq)
    splits = n_seq * rows // extent
    cw = channels // splits // CHUNKS
    f32 = jnp.float32
    vmem = pl.BlockSpec(memory_space=pltpu.VMEM)
    hbm = pl.BlockSpec(memory_space=pl.ANY)
    dma = pltpu.SemaphoreType.DMA
    ff = expand.shape[1]
    out = pl.pallas_call(
        functools.partial(kernel, n_seq, n_dp, rows, splits),
        out_shape=jax.ShapeDtypeStruct((extent, channels), f32),
        in_specs=[hbm] * 7,
        out_specs=vmem,
        scratch_shapes=[
            pltpu.VMEM((extent, channels), f32),
            pltpu.VMEM(norm_gain.shape, f32),
            pltpu.VMEM(filters.shape, f32),
            pltpu.VMEM(level_weights.shape, f32),
            pltpu.VMEM((2 * extent, channels), f32),
            pltpu.VMEM((extent, channels), f32),
            pltpu.VMEM((extent, channels), f32),
            pltpu.VMEM((CHUNKS, n_seq, rows, cw), f32),
            pltpu.VMEM((CHUNKS, n_seq, rows, cw), f32),
            pltpu.VMEM((extent, channels), f32),
            pltpu.VMEM((extent, channels), jnp.bfloat16),
            pltpu.VMEM((extent, channels), jnp.bfloat16),
            pltpu.VMEM((glu.shape[0] * n_dp, glu.shape[1]), f32),
            pltpu.VMEM((expand.shape[0] * n_dp, ff), f32),
            pltpu.VMEM((reduce.shape[0] * n_dp, channels), f32),
            pltpu.VMEM((extent, 2 * channels), f32),
            dma((CHUNKS,)), dma((CHUNKS,)),
            dma((CHUNKS, n_seq)), dma((CHUNKS, n_seq)),
            dma((CHUNKS, n_seq)), dma((CHUNKS, n_seq)),
            dma((CHUNKS,)),
            dma((3, n_dp - 1, 4)), dma((3, n_dp - 1, 4)),
            dma((3,)), dma((4,)),
        ],
        compiler_params=pltpu.CompilerParams(
            collective_id=0, has_side_effects=True, vmem_limit_bytes=60 * 1024 * 1024
        ),
        cost_estimate=pl.CostEstimate(
            flops=6 * extent * channels * (2 * channels + 2 * ff),
            bytes_accessed=4 * (3 * extent * channels), transcendentals=extent * channels * 2,
        ),
    )(features.reshape(extent, channels), norm_gain, filters, level_weights, glu, expand, reduce)
    return out.reshape(batches, extent, channels)


def solution(mesh):
    return jax.shard_map(
        functools.partial(body, mesh.shape["seq"], mesh.shape["dp"]),
        mesh=mesh,
        in_specs=(P("dp", "seq", None), P(), P(), P(), P("dp", None), P("dp", None), P("dp", None)),
        out_specs=P("dp", "seq", None),
        check_vma=False,
    )
```

```python
import functools

import jax
import jax.numpy as jnp
from jax import lax
from jax.experimental import pallas as pl
from jax.experimental.pallas import tpu as pltpu
from jax.sharding import PartitionSpec as P

MESH = pl.DeviceIdType.MESH
LANES = 128
GROUPS = 2
TILE = 256


def split(v):
    hi = v.astype(jnp.bfloat16)
    return hi, (v - hi.astype(jnp.float32)).astype(jnp.bfloat16)


def dot3(a_hi, a_lo, b):
    b_hi, b_lo = split(b)
    f = functools.partial(jnp.dot, preferred_element_type=jnp.float32)
    return f(a_hi, b_hi) + (f(a_hi, b_lo) + f(a_lo, b_hi))


def norm_rows(v, gain_row):
    centred = v - jnp.mean(v, axis=-1, keepdims=True)
    variance = jnp.mean(centred * centred, axis=-1, keepdims=True)
    return centred * lax.rsqrt(variance + 1e-05) * gain_row


def kernel(
    n_seq, n_dp, rows, splits, chunks,
    x_in, gain_in, taps_in, lw_in, glu_ref, expand_ref, reduce_ref, out_ref,
    x_ref, gain_ref, taps_ref, lw_ref, window, level, local, recv1, send2, deep, a_hi_ref, a_lo_ref,
    glu_full, expand_full, reduce_full, proj,
    halo_s, halo_r, a1_s, a1_r, a2_s, a2_r, own_sem, w_s, w_r, w_own, in_sem,
):
    extent, channels = x_ref.shape
    shallow = extent.bit_length() - 1
    deep_levels = n_seq.bit_length() - 1
    all_levels = shallow + deep_levels
    me = lax.axis_index("seq")
    my_dp = lax.axis_index("dp")
    sibling = me + 1 - 2 * lax.rem(me, 2)
    pair = me + 2 - 4 * lax.rem(me // 2, 2)
    g = lax.rem(me, 4)
    hw = channels // chunks
    cw = hw // splits

    def seq_peer(o):
        return lax.rem(me + o, n_seq)

    def dp_peer(o):
        return lax.rem(my_dp + o, n_dp)

    inputs = ((x_in, x_ref), (gain_in, gain_ref), (taps_in, taps_ref), (lw_in, lw_ref))
    copies = [pltpu.make_async_copy(a, b, in_sem.at[i]) for i, (a, b) in enumerate(inputs)]
    for copy in copies:
        copy.start()

    barrier = pltpu.get_barrier_semaphore()

    @pl.loop(1, n_seq)
    def _(o):
        pl.semaphore_signal(barrier, inc=1, device_id={"seq": seq_peer(o)}, device_id_type=MESH)

    for o in range(1, n_dp):
        pl.semaphore_signal(barrier, inc=1, device_id={"dp": dp_peer(o)}, device_id_type=MESH)

    weights = ((glu_ref, glu_full, 4), (expand_ref, expand_full, 4), (reduce_ref, reduce_full, 2))

    def own_shard(w):
        src, full, _ = weights[w]
        height = src.shape[0]
        at = pl.multiple_of(my_dp * height, height)
        return pltpu.make_async_copy(src, full.at[pl.ds(at, height)], w_own.at[w])

    for copy in copies:
        copy.wait()

    @pl.loop(0, extent // 64)
    def _(i):
        at = pl.ds(pl.multiple_of(i * 64, 64), 64)
        to = pl.ds(pl.multiple_of(extent + i * 64, 64), 64)
        window[to, :] = norm_rows(x_ref[at, :], gain_ref[0:1, :])

    @pl.when(me == 0)
    def _():
        window[0:extent, :] = jnp.zeros((extent, channels), jnp.float32)

    pl.semaphore_wait(barrier, n_seq - 1 + n_dp - 1)

    def halo(h):
        cols = slice(h * hw, (h + 1) * hw)
        return pltpu.make_async_remote_copy(
            src_ref=window.at[extent : 2 * extent, cols],
            dst_ref=window.at[0:extent, cols],
            send_sem=halo_s.at[h], recv_sem=halo_r.at[h],
            device_id={"seq": lax.rem(me + 1, n_seq)}, device_id_type=MESH,
        )

    @pl.when(me < n_seq - 1)
    def _():
        for h in range(chunks):
            halo(h).start()

    def piece_rows(w, shard, k):
        height = weights[w][0].shape[0]
        part = height // weights[w][2]
        return pl.ds(pl.multiple_of(shard * height + k * part, part), part)

    def over_dp(w, o):
        src, full, pieces = weights[w]
        part = src.shape[0] // pieces
        mine = lax.rem(g, pieces)
        return pltpu.make_async_remote_copy(
            src_ref=src.at[pl.ds(pl.multiple_of(mine * part, part), part)],
            dst_ref=full.at[piece_rows(w, my_dp, mine)],
            send_sem=w_s.at[w, o - 1, 0], recv_sem=w_r.at[w, o - 1, 0],
            device_id={"dp": dp_peer(o)}, device_id_type=MESH,
        )

    def forward(w, o, kind):
        full = weights[w][1]
        shard = lax.rem(my_dp + n_dp - o, n_dp)
        piece = lax.rem(g + 2, 4) if kind == 3 else lax.rem(g, weights[w][2])
        at = full.at[piece_rows(w, shard, piece)]
        return pltpu.make_async_remote_copy(
            src_ref=at, dst_ref=at,
            send_sem=w_s.at[w, o - 1, kind], recv_sem=w_r.at[w, o - 1, kind],
            device_id={"seq": pair if kind == 1 else sibling}, device_id_type=MESH,
        )

    offsets = range(1, n_dp)

    def stage1(w):
        for o in offsets:
            over_dp(w, o).wait_recv()
            if weights[w][2] == 4:
                forward(w, o, 1).start()
            forward(w, o, 2).start()

    def stage2(w):
        for o in offsets:
            forward(w, o, 1).wait_recv()
            forward(w, o, 3).start()

    def stage3(w):
        for o in offsets:
            forward(w, o, 2).wait_recv()
            if weights[w][2] == 4:
                forward(w, o, 3).wait_recv()

    def send_over_dp(w):
        for o in offsets:
            over_dp(w, o).start()

    send_over_dp(0)
    send_over_dp(1)
    for w in range(3):
        own_shard(w).start()

    def block_of(ref, owner, h):
        at = pl.multiple_of((owner // splits) * rows, rows)
        if splits == 1:
            return ref.at[pl.ds(at, rows), h * cw : (h + 1) * cw]
        lane = pl.multiple_of(h * hw + lax.rem(owner, splits) * cw, LANES)
        return ref.at[pl.ds(at, rows), pl.ds(lane, cw)]

    def out1(h, dest):
        return pltpu.make_async_remote_copy(
            src_ref=block_of(level, dest, h), dst_ref=recv1.at[h, me],
            send_sem=a1_s.at[h, dest], recv_sem=a1_r.at[h, me],
            device_id={"seq": dest}, device_id_type=MESH,
        )

    def in1(h, source):
        return pltpu.make_async_remote_copy(
            src_ref=block_of(level, source, h), dst_ref=recv1.at[h, source],
            send_sem=a1_s.at[h, source], recv_sem=a1_r.at[h, source],
            device_id={"seq": source}, device_id_type=MESH,
        )

    def out2(h, dest):
        return pltpu.make_async_remote_copy(
            src_ref=send2.at[h, dest], dst_ref=block_of(deep, me, h),
            send_sem=a2_s.at[h, dest], recv_sem=a2_r.at[h, me],
            device_id={"seq": dest}, device_id_type=MESH,
        )

    def in2(h, source):
        return pltpu.make_async_remote_copy(
            src_ref=send2.at[h, source], dst_ref=block_of(deep, source, h),
            send_sem=a2_s.at[h, source], recv_sem=a2_r.at[h, source],
            device_id={"seq": source}, device_id_type=MESH,
        )

    for h in range(chunks):

        @pl.when(me > 0)
        def _():
            halo(h).wait_recv()

        @pl.loop(0, hw // LANES)
        def _(c):
            lanes = pl.ds(pl.multiple_of(h * hw + c * LANES, LANES), LANES)
            tap = [taps_ref[i : i + 1, lanes] for i in range(4)]
            current = window[:, lanes]
            total = jnp.zeros((extent, LANES), jnp.float32)
            for step in range(shallow):
                earlier = pltpu.roll(current, 2**step, 0)
                weight = lw_ref[step : step + 1, lanes]
                total = total + (
                    (weight * tap[2]) * earlier[extent:] + (weight * tap[3]) * current[extent:]
                )
                current = tap[0] * earlier + tap[1] * current
            level[:, lanes] = current[extent:]
            local[:, lanes] = total

        own = pltpu.make_async_copy(block_of(level, me, h), recv1.at[h, me], own_sem.at[h])
        own.start()

        @pl.loop(1, n_seq)
        def _(o):
            out1(h, seq_peer(o)).start()

        own.wait()

    stage1(0)
    send_over_dp(2)

    for h in range(chunks):

        @pl.loop(1, n_seq)
        def _(o):
            in1(h, seq_peer(o)).wait_recv()

        @pl.loop(0, cw // LANES)
        def _(c):
            lanes = pl.ds(pl.multiple_of(c * LANES, LANES), LANES)
            first = h * hw + c * LANES
            if splits > 1:
                first = first + lax.rem(me, splits) * cw
            at = pl.ds(pl.multiple_of(first, LANES), LANES)
            tap = [taps_ref[i : i + 1, at][None] for i in range(4)]
            current = recv1[h, :, :, lanes]
            total = jnp.zeros_like(current)
            for step in range(deep_levels):
                shift = 2**step
                earlier = jnp.concatenate(
                    [jnp.zeros((shift, rows, LANES), jnp.float32), current[: n_seq - shift]], axis=0
                )
                weight = lw_ref[shallow + step : shallow + step + 1, at][None]
                total = total + (weight * tap[2]) * earlier + (weight * tap[3]) * current
                current = tap[0] * earlier + tap[1] * current
            total = total + lw_ref[all_levels : all_levels + 1, at][None] * current
            send2[h, :, :, lanes] = total

        own = pltpu.make_async_copy(send2.at[h, me], block_of(deep, me, h), own_sem.at[h])
        own.start()

        @pl.loop(1, n_seq)
        def _(o):
            out2(h, seq_peer(o)).start()

        own.wait()
        if h == chunks // 2 - 1:
            stage2(0)
            stage1(1)

    own_shard(0).wait()
    gw = channels // GROUPS
    per_group = chunks // GROUPS
    for h in range(GROUPS):
        cols = slice(h * gw, (h + 1) * gw)

        for k in range(h * per_group, (h + 1) * per_group):

            @pl.loop(1, n_seq)
            def _(o):
                in2(k, seq_peer(o)).wait_recv()

        @pl.loop(0, extent // 64)
        def _(i):
            at = pl.ds(pl.multiple_of(i * 64, 64), 64)
            v = local[at, cols] + deep[at, cols]
            hi, lo = split(0.5 * v * (1.0 + lax.erf(v * 0.7071067811865476)))
            a_hi_ref[at, cols] = hi
            a_lo_ref[at, cols] = lo

        if h == 0:
            stage3(0)
        if h == GROUPS - 1:
            stage2(1)

        @pl.loop(0, channels // TILE)
        def _(t):
            at = pl.ds(pl.multiple_of(t * TILE, TILE), TILE)
            gate_at = pl.ds(pl.multiple_of(channels + t * TILE, TILE), TILE)
            value = dot3(a_hi_ref[:, cols], a_lo_ref[:, cols], glu_full[cols, at])
            gate = dot3(a_hi_ref[:, cols], a_lo_ref[:, cols], glu_full[cols, gate_at])
            if h > 0:
                value = value + proj[:, at]
                gate = gate + proj[:, gate_at]
            if h < GROUPS - 1:
                proj[:, at] = value
                proj[:, gate_at] = gate
            else:
                out_ref[:, at] = x_ref[:, at] + value * jax.nn.sigmoid(gate)

    stage1(2)

    @pl.loop(0, extent // 64)
    def _(i):
        at = pl.ds(pl.multiple_of(i * 64, 64), 64)
        hi, lo = split(norm_rows(out_ref[at, :], gain_ref[1:2, :]))
        a_hi_ref[at, :] = hi
        a_lo_ref[at, :] = lo

    own_shard(1).wait()
    own_shard(2).wait()
    stage3(1)

    def feed_forward(shard):
        height = reduce_ref.shape[0]

        @pl.loop(0, height // TILE, unroll=min(2, height // TILE))
        def _(t):
            at = pl.ds(pl.multiple_of(shard * height + t * TILE, TILE), TILE)
            hidden = jnp.maximum(dot3(a_hi_ref[...], a_lo_ref[...], expand_full[:, at]), 0.0)
            hi, lo = split(hidden)
            out_ref[...] += dot3(hi, lo, reduce_full[at, :])

    feed_forward(my_dp)
    stage3(2)
    for o in offsets:
        feed_forward(dp_peer(o))

    @pl.when(me < n_seq - 1)
    def _():
        for h in range(chunks):
            halo(h).wait_send()

    for h in range(chunks):

        @pl.loop(1, n_seq)
        def _(o):
            out1(h, seq_peer(o)).wait_send()
            out2(h, seq_peer(o)).wait_send()

    for w in range(3):
        for o in offsets:
            over_dp(w, o).wait_send()
            for kind in (1, 2, 3) if weights[w][2] == 4 else (2,):
                forward(w, o, kind).wait_send()


def body(n_seq, n_dp, features, norm_gain, filters, level_weights, glu, expand, reduce):
    batches, extent, channels = features.shape
    rows = max(8, extent // n_seq)
    splits = n_seq * rows // extent
    chunks = max(GROUPS, channels // LANES // splits)
    cw = channels // splits // chunks
    f32 = jnp.float32
    vmem = pl.BlockSpec(memory_space=pltpu.VMEM)
    hbm = pl.BlockSpec(memory_space=pl.ANY)
    dma = pltpu.SemaphoreType.DMA
    ff = expand.shape[1]
    out = pl.pallas_call(
        functools.partial(kernel, n_seq, n_dp, rows, splits, chunks),
        out_shape=jax.ShapeDtypeStruct((extent, channels), f32),
        in_specs=[hbm] * 7,
        out_specs=vmem,
        scratch_shapes=[
            pltpu.VMEM((extent, channels), f32),
            pltpu.VMEM(norm_gain.shape, f32),
            pltpu.VMEM(filters.shape, f32),
            pltpu.VMEM(level_weights.shape, f32),
            pltpu.VMEM((2 * extent, channels), f32),
            pltpu.VMEM((extent, channels), f32),
            pltpu.VMEM((extent, channels), f32),
            pltpu.VMEM((chunks, n_seq, rows, cw), f32),
            pltpu.VMEM((chunks, n_seq, rows, cw), f32),
            pltpu.VMEM((extent, channels), f32),
            pltpu.VMEM((extent, channels), jnp.bfloat16),
            pltpu.VMEM((extent, channels), jnp.bfloat16),
            pltpu.VMEM((glu.shape[0] * n_dp, glu.shape[1]), f32),
            pltpu.VMEM((expand.shape[0] * n_dp, ff), f32),
            pltpu.VMEM((reduce.shape[0] * n_dp, channels), f32),
            pltpu.VMEM((extent, 2 * channels), f32),
            dma((chunks,)), dma((chunks,)),
            dma((chunks, n_seq)), dma((chunks, n_seq)),
            dma((chunks, n_seq)), dma((chunks, n_seq)),
            dma((chunks,)),
            dma((3, n_dp - 1, 4)), dma((3, n_dp - 1, 4)),
            dma((3,)), dma((4,)),
        ],
        compiler_params=pltpu.CompilerParams(
            collective_id=0, has_side_effects=True, vmem_limit_bytes=60 * 1024 * 1024
        ),
        cost_estimate=pl.CostEstimate(
            flops=6 * extent * channels * (2 * channels + 2 * ff),
            bytes_accessed=4 * (3 * extent * channels), transcendentals=extent * channels * 2,
        ),
    )(features.reshape(extent, channels), norm_gain, filters, level_weights, glu, expand, reduce)
    return out.reshape(batches, extent, channels)


def solution(mesh):
    return jax.shard_map(
        functools.partial(body, mesh.shape["seq"], mesh.shape["dp"]),
        mesh=mesh,
        in_specs=(P("dp", "seq", None), P(), P(), P(), P("dp", None), P("dp", None), P("dp", None)),
        out_specs=P("dp", "seq", None),
        check_vma=False,
    )
```
